32 devices in a mesh: doc: 2 (over y), seq: 8 (over z, core), head: 2 (over x), sub: 1.
Axes of the slice: x: 2, y: 2, z: 4, core: 2. Of those that a mesh axis runs over, the one named last changes fastest.
Arguments:
- tokens: bfloat16 [8192, 4096], P(('doc', 'seq')), parts along dimension 0, may hold values from -6 to 6
- pre_gain: float32 [4096], replicated, may hold values from 0.5 to 1.5
- w_qkv: bfloat16 [3, 4096, 4096], P(None, 'seq', ('head', 'sub')), may hold values from -0.09375 to 0.09375
- level_index: int32 [128, 32, 7], P(('doc', 'seq'), ('head', 'sub')), parts along dimension 0, may hold values from 0 to 7
- head_gain: float32 [4096], P(('head', 'sub')), may hold values from 0.5 to 1.5
- w_out: bfloat16 [4096, 4096], P(('head', 'sub'), 'seq'), may hold values from -0.125 to 0.125
Outputs:
- layer_out: bfloat16 [8192, 4096], P(('doc', 'seq'), ('head', 'sub')), parts along dimension 0
The draws below stay inside these ranges and needn't reach their ends.
There are 2 independent parts, one for each index of `doc`. The reference program is written for one: setup_inputs(seed, part) draws one part's arguments, and reference() takes and returns one part's arrays. A program takes and returns all parts, laid end to end along the dimension named above; an argument that names none is the same for every part. Nothing has to cross between parts.
Inputs may be any that keep to these rules, and one draw needn't show every extreme that they name: `level_index`: indices into the table of eight level weights.
All inputs are finite; a program needn't handle non-finite values.
Results may differ from the reference program's by a relative error of at most 0.015.
Values may be sent and summed in bfloat16 or wider, within the bound.
A program may use at most 128 MiB of HBM per device.

```python
import jax
import jax.numpy as jnp
from jax import lax

D = 4096
HEADS = 32
HD = 128
GROUP = 64
TOKENS = 4096
NCHUNK = 64
LEVELS = 7


def with_ends(result, own_key, least, largest):
    index_at = [jax.random.randint(jax.random.fold_in(own_key, axis), (), 0, length) for axis, length in enumerate(result.shape)]
    main_axis = result.shape.index(max(result.shape))
    neighbour = index_at[:main_axis] + [(index_at[main_axis] + 1) % result.shape[main_axis]] + index_at[main_axis + 1:]
    return result.at[tuple(index_at)].set(least).at[tuple(neighbour)].set(largest)


def with_spikes(entries, rng, source, target, parts, factor):
    def block_of(dim):
        return (jnp.arange(entries.shape[dim]) // (entries.shape[dim] // parts)).reshape((-1,) + (1,) * (entries.ndim - 1 - dim))

    first = jax.random.permutation(rng, parts)[block_of(target)]
    far = (block_of(target) + parts // 2) % parts
    return jnp.where((block_of(source) == first) | (block_of(source) == far), factor * entries, entries)


def steps_of(key, dims, cuts, least, top_value):
    factor_of, own = 1.0, jax.random.fold_in(key, 6)
    for position, parts in cuts:
        draws = jnp.exp(jax.random.uniform(jax.random.fold_in(own, position), (parts,), jnp.float32, least / len(cuts), top_value / len(cuts)))
        factor_of = factor_of * jnp.repeat(draws, dims[position] // parts).reshape([-1 if axis == position else 1 for axis in range(len(dims))])
    return factor_of


def noise(own_key, shape, deviation, reach, split=(), kind=jnp.bfloat16):
    array = jax.random.normal(own_key, shape, jnp.float32) * deviation
    if len(split) > 0:
        array = steps_of(own_key, shape, split, -0.22, 0.18) * array
    return jnp.clip(array, min=-reach, max=reach).astype(kind)


def gaussian_with(key, dims, deviation, most, cuts, heavy, held_as=jnp.bfloat16):
    drawn = deviation * jax.random.normal(key, dims, jnp.float32)
    if cuts:
        drawn = drawn * steps_of(key, dims, cuts, -0.22, 0.18)
    return jnp.clip(with_spikes(drawn, jax.random.fold_in(key, 3), *heavy), -most, most).astype(held_as)


def setup_inputs(seed: int = 0, part: int = 0) -> dict:
    splits = jax.random.split(jax.random.key(seed), 7)
    part_keys = jax.random.split(jax.random.fold_in(splits[6], part), 7)
    return {
        "tokens": noise(part_keys[0], (TOKENS, D), 1.0, 6.0, ((0, 8),)),
        "pre_gain": jnp.clip(jax.random.uniform(splits[1], (D,), jnp.float32, 0.5, 1.5), 0.5, 1.5),
        "w_qkv": noise(splits[2], (3, D, HEADS * HD), D ** -0.5, 0.09375, ((1, 8), (2, 2))),
        "level_index": with_ends(jax.random.randint(part_keys[3], (NCHUNK, HEADS, LEVELS), 0, 8), jax.random.fold_in(part_keys[3], 1), 0, 7).astype(jnp.int32),
        "head_gain": jnp.clip(0.5 + 1.0 * jax.random.uniform(splits[4], (HEADS * HD,), jnp.float32) ** steps_of(splits[4], (HEADS * HD,), ((0, 2),), -0.2, 0.2), 0.5, 1.5),
        "w_out": gaussian_with(splits[5], (HEADS * HD, D), (HEADS * HD) ** -0.5, 0.125, ((0, 2), (1, 8)), (0, 1, 8, 2.0)),
    }


TABLE = (0.25, 0.4, 0.6, 0.8, 1.0, 1.3, 1.7, 2.2)

def bit_length(numbers):
    counted = jnp.zeros_like(numbers)
    for bit_shift in range(16):
        counted = counted + (numbers >> bit_shift > 0).astype(jnp.int32)
    return counted

def reference(tokens, pre_gain, w_qkv, level_index, head_gain, w_out):
    level_table = jnp.asarray(TABLE, dtype=jnp.float32)
    widened = tokens.astype(jnp.float32)
    normed = (widened * lax.rsqrt(lax.optimization_barrier(jnp.mean(widened * widened, axis=1, keepdims=True)) + 1e-05) * pre_gain).astype(jnp.bfloat16)
    queries = jnp.dot(normed, w_qkv[0], preferred_element_type=jnp.float32).astype(jnp.bfloat16)
    key_rows = jnp.dot(normed, w_qkv[1], preferred_element_type=jnp.float32).astype(jnp.bfloat16)
    values = jnp.dot(normed, w_qkv[2], preferred_element_type=jnp.float32).astype(jnp.bfloat16)
    group_ids = jnp.arange(NCHUNK, dtype=jnp.int32)
    later_group = group_ids[:, None]
    earlier_group = group_ids[None, :]
    level_of = bit_length(jnp.bitwise_xor(later_group, earlier_group)).astype(jnp.int32)
    before = earlier_group < later_group
    positions = jnp.arange(GROUP, dtype=jnp.int32)
    causal = positions[:, None] >= positions[None, :]
    scaling = HD ** (-0.5)

    def heads_first(matrix):
        return matrix.reshape(NCHUNK, GROUP, HEADS, HD).transpose(2, 0, 1, 3)

    def one_head(inputs):
        head_query, head_keys, head_values, head_index, head_scale = inputs
        level_weight = level_table[head_index]
        coefficient = jnp.where(before, jnp.take_along_axis(level_weight, level_of, axis=1), 0.0)
        query_wide = head_query.astype(jnp.float32)
        keys_wide = head_keys.astype(jnp.float32)
        values_wide = head_values.astype(jnp.float32)
        states = jnp.einsum('cti,ctj->cij', keys_wide, values_wide)
        carried = jnp.einsum('cj,jab->cab', coefficient, states, precision=lax.Precision.HIGHEST)
        scores = jnp.einsum('cti,cui->ctu', query_wide, keys_wide)
        weights = (scores * scaling * level_weight[:, 0][:, None, None] * causal).astype(jnp.bfloat16)
        local_part = jnp.einsum('ctu,cui->cti', weights.astype(jnp.float32), values_wide)
        carried_part = jnp.einsum('cti,cij->ctj', query_wide, carried, precision=lax.Precision.HIGHEST) * scaling
        attended = local_part + carried_part
        head_normed = attended * lax.rsqrt(lax.optimization_barrier(jnp.mean(attended * attended, axis=2, keepdims=True)) + 1e-05) * head_scale
        return head_normed.astype(jnp.bfloat16).reshape(TOKENS, HD)
    per_head = lax.map(one_head, (heads_first(queries), heads_first(key_rows), heads_first(values), level_index.transpose(1, 0, 2), head_gain.reshape(HEADS, HD)))
    head_normed = per_head.transpose(1, 0, 2).reshape(TOKENS, HEADS * HD)
    return (widened + jnp.dot(head_normed, w_out, preferred_element_type=jnp.float32)).astype(jnp.bfloat16)
```

```python
import functools

import jax
import jax.numpy as jnp
from jax import lax
from jax.experimental import pallas as pl
from jax.experimental.pallas import tpu as pltpu
from jax.sharding import PartitionSpec as P

HD = 128
GROUP = 64


TABLE = (0.25, 0.4, 0.6, 0.8, 1.0, 1.3, 1.7, 2.2)


def partner_2(value, axis, apart):
    mask = 2**apart
    pairs = [(source, source ^ mask) for source in range(lax.axis_size(axis))]
    return lax.ppermute(value, axis, pairs)


def bit_length(numbers):
    counted = jnp.zeros_like(numbers)
    for bit_shift in range(16):
        counted = counted + (numbers >> bit_shift > 0).astype(jnp.int32)
    return counted


def head_rows(local_bits, query, keys, values, row_weight, partners, gain):
    rows = query.shape[0]
    scores = lax.dot_general(
        query, keys, (((1,), (1,)), ((), ())), preferred_element_type=jnp.float32
    )
    later = lax.broadcasted_iota(jnp.int32, (rows, rows), 0)
    earlier = lax.broadcasted_iota(jnp.int32, (rows, rows), 1)
    apart = later ^ earlier
    factor = row_weight[:, local_bits : local_bits + 1]
    for level in range(local_bits - 1, -1, -1):
        factor = jnp.where(apart < GROUP << level, row_weight[:, level : level + 1], factor)
    weights = jnp.where(later >= earlier, scores * factor, 0.0).astype(jnp.bfloat16)
    attended = jnp.dot(weights, values, preferred_element_type=jnp.float32)
    for bit_index, partner in enumerate(partners):
        level = local_bits + 1 + bit_index
        attended += row_weight[:, level : level + 1] * jnp.dot(
            query, partner, preferred_element_type=jnp.float32
        )
    mean_square = jnp.mean(attended * attended, axis=1, keepdims=True)
    return (attended * lax.rsqrt(mean_square + 1e-05) * gain).astype(jnp.bfloat16)


def head_kernel(local_bits, q_ref, k_ref, v_ref, weight_ref, partner_ref, gain_ref, out_ref):
    out_ref[...] = head_rows(
        local_bits,
        q_ref[...],
        k_ref[...],
        v_ref[...],
        weight_ref[0],
        [partner_ref[n, 0] for n in range(partner_ref.shape[0])],
        gain_ref[...],
    )


def gathered(weight, axis):
    docs = lax.axis_size("doc")
    part = weight.shape[axis] // docs
    mine = lax.dynamic_slice_in_dim(weight, lax.axis_index("doc") * part, part, axis)
    return lax.all_gather(mine, ("doc", "seq"), axis=0)


def body(tokens, pre_gain, w_qkv, level_index, head_gain, w_out):
    tok_rows, width = tokens.shape
    docs, seqs = lax.axis_size("doc"), lax.axis_size("seq")
    widened = tokens.astype(jnp.float32)
    normed = (
        widened * lax.rsqrt(jnp.mean(widened * widened, axis=1, keepdims=True) + 1e-05) * pre_gain
    ).astype(jnp.bfloat16)
    head_cols = w_qkv.shape[2]
    groups_here = tok_rows // GROUP
    swapped = normed.reshape(tok_rows, seqs, docs, -1).swapaxes(1, 2).reshape(tok_rows, width)

    def project(which):
        matrix = gathered(w_qkv[which], 0).reshape(width, head_cols)
        return jnp.dot(swapped, matrix, preferred_element_type=jnp.float32).astype(jnp.bfloat16)

    key_rows, values, queries = project(1), project(2), project(0)
    w_out, _ = lax.optimization_barrier((w_out, values))
    out_matrix = gathered(w_out, 0)
    return attend(
        widened, queries, key_rows, values, level_index, head_gain, out_matrix, groups_here
    )


def attend(widened, queries, key_rows, values, level_index, head_gain, out_matrix, groups_here):
    tok_rows = queries.shape[0]
    heads_here = queries.shape[1] // HD
    level_weight = jnp.zeros(level_index.shape, jnp.float32)
    for entry in range(len(TABLE)):
        level_weight = level_weight + jnp.where(level_index == entry, TABLE[entry], 0.0)
    totals = jnp.einsum(
        "thi,thj->hij",
        key_rows.reshape(tok_rows, heads_here, HD),
        values.reshape(tok_rows, heads_here, HD),
        preferred_element_type=jnp.float32,
    )
    local_bits = groups_here.bit_length() - 1
    seq_bits = lax.axis_size("seq").bit_length() - 1
    position = lax.axis_index("seq")
    partners = []
    block_sum = totals
    for bit_index in range(seq_bits):
        partner = partner_2(block_sum.astype(jnp.bfloat16), "seq", bit_index)
        partners.append(partner)
        block_sum = block_sum + partner.astype(jnp.float32)
    bits = jnp.arange(seq_bits, dtype=jnp.int32)
    used = jnp.concatenate(
        [jnp.ones((local_bits + 1,), jnp.int32), position >> bits & 1]
    ).astype(jnp.float32) * HD ** (-0.5)
    row_weights = jnp.repeat((level_weight * used).swapaxes(0, 1), GROUP, axis=1)
    head_normed = pl.pallas_call(
        functools.partial(head_kernel, local_bits),
        grid=(heads_here,),
        in_specs=[pl.BlockSpec((tok_rows, HD), lambda h: (0, h))] * 3
        + [
            pl.BlockSpec((1,) + row_weights.shape[1:], lambda h: (h, 0, 0)),
            pl.BlockSpec((seq_bits, 1, HD, HD), lambda h: (0, h, 0, 0)),
            pl.BlockSpec((1, HD), lambda h: (0, h)),
        ],
        out_specs=pl.BlockSpec((tok_rows, HD), lambda h: (0, h)),
        out_shape=jax.ShapeDtypeStruct((tok_rows, heads_here * HD), jnp.bfloat16),
        compiler_params=pltpu.CompilerParams(vmem_limit_bytes=32 * 2**20),
        cost_estimate=pl.CostEstimate(
            flops=heads_here * tok_rows * HD * 4 * (tok_rows + HD * seq_bits),
            bytes_accessed=tok_rows * heads_here * HD * 12,
            transcendentals=0,
        ),
    )(queries, key_rows, values, row_weights, jnp.stack(partners), head_gain[None, :])
    docs = lax.axis_size("doc")
    split_rows = head_normed.reshape(tok_rows, docs, heads_here * HD // docs)
    local_terms = jnp.einsum(
        "tyk,yskc->tsc",
        split_rows,
        out_matrix.reshape(docs, -1, *out_matrix.shape[1:]),
        preferred_element_type=jnp.float32,
    ).reshape(tok_rows, -1)
    feature_cols = local_terms.shape[1] // lax.axis_size(("head", "sub"))
    summed = lax.psum_scatter(
        local_terms.astype(jnp.bfloat16), ("head", "sub"), scatter_dimension=1, tiled=True
    ).astype(jnp.float32)
    residual = lax.dynamic_slice_in_dim(
        widened, lax.axis_index(("head", "sub")) * feature_cols, feature_cols, 1
    )
    return (residual + summed).astype(jnp.bfloat16)


def solution(mesh):
    placed = (
        P(("doc", "seq"), None),
        P(),
        P(None, "seq", ("head", "sub")),
        P(("doc", "seq"), ("head", "sub"), None),
        P(("head", "sub")),
        P(("head", "sub"), "seq"),
    )
    return jax.shard_map(
        body,
        mesh=mesh,
        in_specs=placed,
        out_specs=P(("doc", "seq"), ("head", "sub")),
        check_vma=False,
    )
```

```python
import functools

import jax
import jax.numpy as jnp
from jax import lax
from jax.experimental import pallas as pl
from jax.experimental.pallas import tpu as pltpu
from jax.sharding import PartitionSpec as P

HD = 128
GROUP = 64


TABLE = (0.25, 0.4, 0.6, 0.8, 1.0, 1.3, 1.7, 2.2)


def partner_2(value, axis, apart):
    mask = 2**apart
    pairs = [(source, source ^ mask) for source in range(lax.axis_size(axis))]
    return lax.ppermute(value, axis, pairs)


def bit_length(numbers):
    counted = jnp.zeros_like(numbers)
    for bit_shift in range(16):
        counted = counted + (numbers >> bit_shift > 0).astype(jnp.int32)
    return counted


def head_rows(local_bits, query, keys, values, row_weight, partners, gain):
    rows = query.shape[0]
    scores = lax.dot_general(
        query, keys, (((1,), (1,)), ((), ())), preferred_element_type=jnp.float32
    )
    later = lax.broadcasted_iota(jnp.int32, (rows, rows), 0)
    earlier = lax.broadcasted_iota(jnp.int32, (rows, rows), 1)
    apart = later ^ earlier
    factor = row_weight[:, local_bits : local_bits + 1]
    for level in range(local_bits - 1, -1, -1):
        factor = jnp.where(apart < GROUP << level, row_weight[:, level : level + 1], factor)
    weights = jnp.where(later >= earlier, scores * factor, 0.0).astype(jnp.bfloat16)
    attended = jnp.dot(weights, values, preferred_element_type=jnp.float32)
    for bit_index, partner in enumerate(partners):
        level = local_bits + 1 + bit_index
        attended += row_weight[:, level : level + 1] * jnp.dot(
            query, partner, preferred_element_type=jnp.float32
        )
    mean_square = jnp.mean(attended * attended, axis=1, keepdims=True)
    return (attended * lax.rsqrt(mean_square + 1e-05) * gain).astype(jnp.bfloat16)


def head_block(which, head):
    return which, 0, head


def head_kernel(local_bits, q_ref, k_ref, v_ref, weight_ref, partner_ref, gain_ref, out_ref):
    out_ref[...] = head_rows(
        local_bits,
        q_ref[0],
        k_ref[0],
        v_ref[0],
        weight_ref[0],
        [partner_ref[n, 0] for n in range(partner_ref.shape[0])],
        gain_ref[...],
    )


MESH = pl.DeviceIdType.MESH


def spread_kernel(lanes, pieces, w_ref, out_ref, zr, yr, cr, down, up, ys, cs, own):
    docs_at, seq_at = lax.axis_index("doc"), lax.axis_index("seq")
    line = lax.axis_size("seq") // lanes
    z, lane = seq_at // lanes, seq_at % lanes
    units = w_ref.shape[0] * pieces
    half_rows = w_ref.shape[1] // 2
    rows = half_rows // pieces
    count = (line - 1) * units

    def row_slice(unit, half):
        start = half * half_rows + unit % pieces * rows
        return pl.ds(pl.multiple_of(start, 16), rows)

    def slot(source, unit, half):
        return out_ref.at[unit // pieces, source * lanes + lane, row_slice(unit, half)]

    def shard(unit, half):
        return w_ref.at[unit // pieces, row_slice(unit, half)]

    def z_copy(source, unit, is_own, step, send):
        src = shard(unit, docs_at) if is_own else slot(source, unit, docs_at)
        return pltpu.make_async_remote_copy(
            src, slot(source, unit, docs_at), send.at[source, unit], zr.at[source, unit],
            device_id={"seq": seq_at + step * lanes}, device_id_type=MESH,
        )

    def y_copy(source, unit, half):
        return pltpu.make_async_remote_copy(
            slot(source, unit, half), slot(source, unit, half), ys.at[source, unit],
            yr.at[source, unit], device_id={"doc": 1 - docs_at}, device_id_type=MESH,
        )

    def core_copy(source, unit, half, is_own):
        src = shard(unit, half) if is_own else slot(source, unit, half)
        return pltpu.make_async_remote_copy(
            src, slot(source, unit, half), cs.at[source, unit, half], cr.at[source, unit, half],
            device_id={"seq": z * lanes + (lanes - 1 - lane)}, device_id_type=MESH,
        )

    def core_arrival(source, unit, half):
        there = out_ref.at[unit // pieces, source * lanes + (lanes - 1 - lane), row_slice(unit, half)]
        return pltpu.make_async_remote_copy(
            there, there, cs.at[source, unit, half], cr.at[source, unit, half],
            device_id={"seq": z * lanes + (lanes - 1 - lane)}, device_id_type=MESH,
        )

    barrier = pltpu.get_barrier_semaphore()

    def greet(**where):
        pl.semaphore_signal(barrier, inc=1, device_id=where, device_id_type=MESH)

    pl.when(z > 0)(lambda: greet(seq=seq_at - lanes))
    pl.when(z < line - 1)(lambda: greet(seq=seq_at + lanes))
    greet(doc=1 - docs_at)
    if lanes == 2:
        greet(seq=z * lanes + (lanes - 1 - lane))
    edges = (z > 0).astype(jnp.int32) + (z < line - 1).astype(jnp.int32)
    pl.semaphore_wait(barrier, edges + lanes)

    own_copies = [
        pltpu.make_async_copy(w_ref.at[k], out_ref.at[k, seq_at], own.at[k])
        for k in range(w_ref.shape[0])
    ]

    def sends(position, begin):
        unit, hop = position % units, position // units
        for step, send in ((-1, down), (1, up)):
            source = z - step * hop
            target = z + step
            there = (target >= 0) & (target < line)
            there = there & (source >= 0) & (source < line)
            there = there & (position >= 0) & (position < count)
            for is_own in (True, False):
                first = (hop == 0) if is_own else (hop > 0)

                @pl.when(there & first)
                def _():
                    copy = z_copy(source, unit, is_own, step, send)
                    copy.start() if begin else copy.wait_send()

    def arrivals(position, act):
        unit, hop = position % units, position // units
        for step in (-1, 1):
            source = z - step * (hop + 1)
            there = (source >= 0) & (source < line) & (position >= 0) & (position < count)

            @pl.when(there)
            def _():
                act(source, unit, step)

    def on_z(source, unit, step):
        z_copy(source, unit, False, -step, down).wait_recv()
        y_copy(source, unit, docs_at).start()
        if lanes == 2:
            core_copy(source, unit, docs_at, False).start()

    def on_y(source, unit, step):
        y_copy(source, unit, 1 - docs_at).wait_recv()
        if lanes == 2:
            core_copy(source, unit, 1 - docs_at, False).start()

    lag = jnp.where((z == 0) | (z == line - 1), 1, units)

    def turn(t, carry):
        sends(t - 2, False)
        sends(t, True)
        arrivals(t - 2, on_z)
        arrivals(t - 2 - lag, on_y)

        @pl.when(t == 1)
        def _():
            for copy in own_copies:
                copy.start()

        if lanes == 2:

            @pl.when(t < units)
            def _():
                core_copy(z, t, 0, True).start()
                core_copy(z, t, 1, True).start()

        return carry

    lax.fori_loop(0, count + 2 + units, turn, 0)

    def finish(n, carry):
        source, unit = n // units, n % units
        pl.when(source != z)(lambda: y_copy(source, unit, docs_at).wait_send())
        if lanes == 2:
            for half in (0, 1):
                core_arrival(source, unit, half).wait_recv()
                core_copy(source, unit, half, False).wait_send()
        return carry

    lax.fori_loop(0, line * units, finish, 0)
    for copy in own_copies:
        copy.wait()


def spread(w_qkv):
    seqs = lax.axis_size("seq")
    lanes = 2 if lax.axis_size("sub") == 1 and seqs % 2 == 0 else 1
    line = seqs // lanes
    pieces = 2 if line <= 4 else 1
    units = w_qkv.shape[0] * pieces
    sem = pltpu.SemaphoreType.DMA
    core = (line, units, 2) if lanes == 2 else (1, 1, 1)
    return pl.pallas_call(
        functools.partial(spread_kernel, lanes, pieces),
        out_shape=jax.ShapeDtypeStruct(
            (w_qkv.shape[0], seqs) + w_qkv.shape[1:], jnp.bfloat16
        ),
        in_specs=[pl.BlockSpec(memory_space=pl.ANY)],
        out_specs=pl.BlockSpec(memory_space=pl.ANY),
        scratch_shapes=[sem((line, units)), sem((line, units)), sem(core)]
        + [sem((line, units))] * 3
        + [sem(core), sem((w_qkv.shape[0],))],
        compiler_params=pltpu.CompilerParams(collective_id=0, has_side_effects=True),
    )(w_qkv)


def gathered(weight, axis):
    docs = lax.axis_size("doc")
    part = weight.shape[axis] // docs
    mine = lax.dynamic_slice_in_dim(weight, lax.axis_index("doc") * part, part, axis)
    return lax.all_gather(mine, ("doc", "seq"), axis=0)


def body(tokens, pre_gain, w_qkv, level_index, head_gain, w_out):
    tok_rows, width = tokens.shape
    docs, seqs = lax.axis_size("doc"), lax.axis_size("seq")
    widened = tokens.astype(jnp.float32)
    normed = (
        widened * lax.rsqrt(jnp.mean(widened * widened, axis=1, keepdims=True) + 1e-05) * pre_gain
    ).astype(jnp.bfloat16)
    head_cols = w_qkv.shape[2]
    groups_here = tok_rows // GROUP
    if docs == 2 and seqs > 1:
        every = spread(w_qkv)
    else:
        every = lax.all_gather(w_qkv, "seq", axis=1)
    w_out, every = lax.optimization_barrier((w_out, every))
    out_matrix = gathered(w_out, 0)
    projected = jnp.einsum(
        "td,kdc->ktc",
        normed,
        every.reshape(-1, width, head_cols),
        preferred_element_type=jnp.float32,
    ).astype(jnp.bfloat16)
    return attend(widened, projected, level_index, head_gain, out_matrix, groups_here)


def attend(widened, projected, level_index, head_gain, out_matrix, groups_here):
    tok_rows = projected.shape[1]
    heads_here = projected.shape[2] // HD
    level_weight = jnp.zeros(level_index.shape, jnp.float32)
    for entry in range(len(TABLE)):
        level_weight = level_weight + jnp.where(level_index == entry, TABLE[entry], 0.0)
    totals = jnp.einsum(
        "thi,thj->hij",
        projected[1].reshape(tok_rows, heads_here, HD),
        projected[2].reshape(tok_rows, heads_here, HD),
        preferred_element_type=jnp.float32,
    )
    local_bits = groups_here.bit_length() - 1
    seq_bits = lax.axis_size("seq").bit_length() - 1
    position = lax.axis_index("seq")
    partners = []
    block_sum = totals
    for bit_index in range(seq_bits):
        partner = partner_2(block_sum.astype(jnp.bfloat16), "seq", bit_index)
        partners.append(partner)
        block_sum = block_sum + partner.astype(jnp.float32)
    bits = jnp.arange(seq_bits, dtype=jnp.int32)
    used = jnp.concatenate(
        [jnp.ones((local_bits + 1,), jnp.int32), position >> bits & 1]
    ).astype(jnp.float32) * HD ** (-0.5)
    row_weights = jnp.repeat((level_weight * used).swapaxes(0, 1), GROUP, axis=1)
    head_normed = pl.pallas_call(
        functools.partial(head_kernel, local_bits),
        grid=(heads_here,),
        in_specs=[
            pl.BlockSpec((1, tok_rows, HD), functools.partial(head_block, k)) for k in range(3)
        ]
        + [
            pl.BlockSpec((1,) + row_weights.shape[1:], lambda h: (h, 0, 0)),
            pl.BlockSpec((seq_bits, 1, HD, HD), lambda h: (0, h, 0, 0)),
            pl.BlockSpec((1, HD), lambda h: (0, h)),
        ],
        out_specs=pl.BlockSpec((tok_rows, HD), lambda h: (0, h)),
        out_shape=jax.ShapeDtypeStruct((tok_rows, heads_here * HD), jnp.bfloat16),
        compiler_params=pltpu.CompilerParams(vmem_limit_bytes=32 * 2**20),
        cost_estimate=pl.CostEstimate(
            flops=heads_here * tok_rows * HD * 4 * (tok_rows + HD * seq_bits),
            bytes_accessed=tok_rows * heads_here * HD * 12,
            transcendentals=0,
        ),
    )(projected, projected, projected, row_weights, jnp.stack(partners), head_gain[None, :])
    docs = lax.axis_size("doc")
    split_rows = head_normed.reshape(tok_rows, docs, heads_here * HD // docs)
    local_terms = jnp.einsum(
        "tyk,yskc->tsc",
        split_rows,
        out_matrix.reshape(docs, -1, *out_matrix.shape[1:]),
        preferred_element_type=jnp.float32,
    ).reshape(tok_rows, -1)
    feature_cols = local_terms.shape[1] // lax.axis_size(("head", "sub"))
    summed = lax.psum_scatter(
        local_terms.astype(jnp.bfloat16), ("head", "sub"), scatter_dimension=1, tiled=True
    ).astype(jnp.float32)
    residual = lax.dynamic_slice_in_dim(
        widened, lax.axis_index(("head", "sub")) * feature_cols, feature_cols, 1
    )
    return (residual + summed).astype(jnp.bfloat16)


def solution(mesh):
    placed = (
        P(("doc", "seq"), None),
        P(),
        P(None, "seq", ("head", "sub")),
        P(("doc", "seq"), ("head", "sub"), None),
        P(("head", "sub")),
        P(("head", "sub"), "seq"),
    )
    return jax.shard_map(
        body,
        mesh=mesh,
        in_specs=placed,
        out_specs=P(("doc", "seq"), ("head", "sub")),
        check_vma=False,
    )
```

```python
import functools

import jax
import jax.numpy as jnp
from jax import lax
from jax.experimental import pallas as pl
from jax.experimental.pallas import tpu as pltpu
from jax.sharding import PartitionSpec as P

HD = 128
GROUP = 64


TABLE = (0.25, 0.4, 0.6, 0.8, 1.0, 1.3, 1.7, 2.2)


def partner_2(value, axis, apart):
    mask = 2**apart
    pairs = [(source, source ^ mask) for source in range(lax.axis_size(axis))]
    return lax.ppermute(value, axis, pairs)


def bit_length(numbers):
    counted = jnp.zeros_like(numbers)
    for bit_shift in range(16):
        counted = counted + (numbers >> bit_shift > 0).astype(jnp.int32)
    return counted


def head_rows(local_bits, query, keys, values, row_weight, partners, gain):
    rows = query.shape[0]
    scores = lax.dot_general(
        query, keys, (((1,), (1,)), ((), ())), preferred_element_type=jnp.float32
    )
    later = lax.broadcasted_iota(jnp.int32, (rows, rows), 0)
    earlier = lax.broadcasted_iota(jnp.int32, (rows, rows), 1)
    apart = later ^ earlier
    factor = row_weight[:, local_bits : local_bits + 1]
    for level in range(local_bits - 1, -1, -1):
        factor = jnp.where(apart < GROUP << level, row_weight[:, level : level + 1], factor)
    weights = jnp.where(later >= earlier, scores * factor, 0.0).astype(jnp.bfloat16)
    attended = jnp.dot(weights, values, preferred_element_type=jnp.float32)
    for bit_index, partner in enumerate(partners):
        level = local_bits + 1 + bit_index
        attended += row_weight[:, level : level + 1] * jnp.dot(
            query, partner, preferred_element_type=jnp.float32
        )
    mean_square = jnp.mean(attended * attended, axis=1, keepdims=True)
    return (attended * lax.rsqrt(mean_square + 1e-05) * gain).astype(jnp.bfloat16)


def head_block(which, head):
    return which, 0, head


def head_kernel(local_bits, q_ref, k_ref, v_ref, weight_ref, partner_ref, gain_ref, out_ref):
    out_ref[...] = head_rows(
        local_bits,
        q_ref[0],
        k_ref[0],
        v_ref[0],
        weight_ref[0],
        [partner_ref[n, 0] for n in range(partner_ref.shape[0])],
        gain_ref[...],
    )


MESH = pl.DeviceIdType.MESH


def spread_kernel(lanes, pieces, w_ref, out_ref, zr, yr, cr, down, up, ys, cs, own):
    docs_at, seq_at = lax.axis_index("doc"), lax.axis_index("seq")
    line = lax.axis_size("seq") // lanes
    z, lane = seq_at // lanes, seq_at % lanes
    units = w_ref.shape[0] * pieces
    half_rows = w_ref.shape[1] // 2
    rows = half_rows // pieces
    count = (line - 1) * units

    def row_slice(unit, half):
        start = half * half_rows + unit % pieces * rows
        return pl.ds(pl.multiple_of(start, 16), rows)

    def slot(source, unit, half):
        return out_ref.at[unit // pieces, source * lanes + lane, row_slice(unit, half)]

    def shard(unit, half):
        return w_ref.at[unit // pieces, row_slice(unit, half)]

    def z_copy(source, unit, is_own, step, send):
        src = shard(unit, docs_at) if is_own else slot(source, unit, docs_at)
        return pltpu.make_async_remote_copy(
            src, slot(source, unit, docs_at), send.at[source, unit], zr.at[source, unit],
            device_id={"seq": seq_at + step * lanes}, device_id_type=MESH,
        )

    def y_copy(source, unit, half):
        return pltpu.make_async_remote_copy(
            slot(source, unit, half), slot(source, unit, half), ys.at[source, unit],
            yr.at[source, unit], device_id={"doc": 1 - docs_at}, device_id_type=MESH,
        )

    def core_copy(source, unit, half, is_own):
        src = shard(unit, half) if is_own else slot(source, unit, half)
        return pltpu.make_async_remote_copy(
            src, slot(source, unit, half), cs.at[source, unit, half], cr.at[source, unit, half],
            device_id={"seq": z * lanes + (lanes - 1 - lane)}, device_id_type=MESH,
        )

    def core_arrival(source, unit, half):
        there = out_ref.at[unit // pieces, source * lanes + (lanes - 1 - lane), row_slice(unit, half)]
        return pltpu.make_async_remote_copy(
            there, there, cs.at[source, unit, half], cr.at[source, unit, half],
            device_id={"seq": z * lanes + (lanes - 1 - lane)}, device_id_type=MESH,
        )

    barrier = pltpu.get_barrier_semaphore()

    def greet(**where):
        pl.semaphore_signal(barrier, inc=1, device_id=where, device_id_type=MESH)

    pl.when(z > 0)(lambda: greet(seq=seq_at - lanes))
    pl.when(z < line - 1)(lambda: greet(seq=seq_at + lanes))
    greet(doc=1 - docs_at)
    if lanes == 2:
        greet(seq=z * lanes + (lanes - 1 - lane))
    edges = (z > 0).astype(jnp.int32) + (z < line - 1).astype(jnp.int32)
    pl.semaphore_wait(barrier, edges + lanes)

    own_copies = [
        pltpu.make_async_copy(w_ref.at[k], out_ref.at[k, seq_at], own.at[k])
        for k in range(w_ref.shape[0])
    ]

    def sends(position, begin):
        unit, hop = position % units, position // units
        for step, send in ((-1, down), (1, up)):
            source = z - step * hop
            target = z + step
            there = (target >= 0) & (target < line)
            there = there & (source >= 0) & (source < line)
            there = there & (position >= 0) & (position < count)
            for is_own in (True, False):
                first = (hop == 0) if is_own else (hop > 0)

                @pl.when(there & first)
                def _():
                    copy = z_copy(source, unit, is_own, step, send)
                    copy.start() if begin else copy.wait_send()

    def arrivals(position, act):
        unit, hop = position % units, position // units
        for step in (-1, 1):
            source = z - step * (hop + 1)
            there = (source >= 0) & (source < line) & (position >= 0) & (position < count)

            @pl.when(there)
            def _():
                act(source, unit, step)

    def on_z(source, unit, step):
        z_copy(source, unit, False, -step, down).wait_recv()
        y_copy(source, unit, docs_at).start()
        if lanes == 2:
            core_copy(source, unit, docs_at, False).start()

    def on_y(source, unit, step):
        y_copy(source, unit, 1 - docs_at).wait_recv()
        if lanes == 2:
            core_copy(source, unit, 1 - docs_at, False).start()

    lag = jnp.where((z == 0) | (z == line - 1), 1, units)

    def turn(t, carry):
        sends(t - 2, False)
        sends(t, True)
        arrivals(t - 2, on_z)
        arrivals(t - 2 - lag, on_y)

        @pl.when(t == 1)
        def _():
            for copy in own_copies:
                copy.start()

        if lanes == 2:

            @pl.when(t < units)
            def _():
                core_copy(z, t, 0, True).start()
                core_copy(z, t, 1, True).start()

        return carry

    lax.fori_loop(0, count + 2 + units, turn, 0)

    def finish(n, carry):
        source, unit = n // units, n % units
        pl.when(source != z)(lambda: y_copy(source, unit, docs_at).wait_send())
        if lanes == 2:
            for half in (0, 1):
                core_arrival(source, unit, half).wait_recv()
                core_copy(source, unit, half, False).wait_send()
        return carry

    lax.fori_loop(0, line * units, finish, 0)
    for copy in own_copies:
        copy.wait()


def spread(w_qkv):
    seqs = lax.axis_size("seq")
    lanes = 2 if lax.axis_size("sub") == 1 and seqs % 2 == 0 else 1
    line = seqs // lanes
    pieces = 2 if line <= 4 else 1
    units = w_qkv.shape[0] * pieces
    sem = pltpu.SemaphoreType.DMA
    core = (line, units, 2) if lanes == 2 else (1, 1, 1)
    return pl.pallas_call(
        functools.partial(spread_kernel, lanes, pieces),
        out_shape=jax.ShapeDtypeStruct(
            (w_qkv.shape[0], seqs) + w_qkv.shape[1:], jnp.bfloat16
        ),
        in_specs=[pl.BlockSpec(memory_space=pl.ANY)],
        out_specs=pl.BlockSpec(memory_space=pl.ANY),
        scratch_shapes=[sem((line, units)), sem((line, units)), sem(core)]
        + [sem((line, units))] * 3
        + [sem(core), sem((w_qkv.shape[0],))],
        compiler_params=pltpu.CompilerParams(collective_id=0, has_side_effects=True),
    )(w_qkv)


def gathered_columns(w_out):
    docs = lax.axis_size("doc")
    part = w_out.shape[1] // docs
    mine = lax.dynamic_slice_in_dim(w_out, lax.axis_index("doc") * part, part, 1)
    return lax.all_gather(mine.T, ("seq", "doc"), axis=0, tiled=True)


def body(tokens, pre_gain, w_qkv, level_index, head_gain, w_out):
    tok_rows, width = tokens.shape
    docs, seqs = lax.axis_size("doc"), lax.axis_size("seq")
    widened = tokens.astype(jnp.float32)
    normed = (
        widened * lax.rsqrt(jnp.mean(widened * widened, axis=1, keepdims=True) + 1e-05) * pre_gain
    ).astype(jnp.bfloat16)
    head_cols = w_qkv.shape[2]
    groups_here = tok_rows // GROUP
    if docs == 2 and seqs > 1:
        every = spread(w_qkv)
    else:
        every = lax.all_gather(w_qkv, "seq", axis=1)
    w_out, every = lax.optimization_barrier((w_out, every))
    out_matrix = gathered_columns(w_out)
    projected = jnp.einsum(
        "td,kdc->ktc",
        normed,
        every.reshape(-1, width, head_cols),
        preferred_element_type=jnp.float32,
    ).astype(jnp.bfloat16)
    return attend(widened, projected, level_index, head_gain, out_matrix, groups_here)


def attend(widened, projected, level_index, head_gain, out_matrix, groups_here):
    tok_rows = projected.shape[1]
    heads_here = projected.shape[2] // HD
    level_weight = jnp.zeros(level_index.shape, jnp.float32)
    for entry in range(len(TABLE)):
        level_weight = level_weight + jnp.where(level_index == entry, TABLE[entry], 0.0)
    totals = jnp.einsum(
        "thi,thj->hij",
        projected[1].reshape(tok_rows, heads_here, HD),
        projected[2].reshape(tok_rows, heads_here, HD),
        preferred_element_type=jnp.float32,
    )
    local_bits = groups_here.bit_length() - 1
    seq_bits = lax.axis_size("seq").bit_length() - 1
    position = lax.axis_index("seq")
    partners = []
    block_sum, rounded = totals, totals.astype(jnp.bfloat16)
    for bit_index in range(seq_bits):
        if bit_index == seq_bits - 1 and bit_index > 0:
            near = partner_2(previous, "seq", bit_index)
            far = lax.ppermute(
                previous,
                "seq",
                [(n, n ^ (3 << bit_index - 1)) for n in range(lax.axis_size("seq"))],
            )
            summed = near.astype(jnp.float32) + far.astype(jnp.float32)
            partners.append(summed.astype(jnp.bfloat16))
        else:
            partner = partner_2(rounded, "seq", bit_index)
            partners.append(partner)
            previous = rounded
            block_sum = block_sum + partner.astype(jnp.float32)
            rounded = block_sum.astype(jnp.bfloat16)
    bits = jnp.arange(seq_bits, dtype=jnp.int32)
    used = jnp.concatenate(
        [jnp.ones((local_bits + 1,), jnp.int32), position >> bits & 1]
    ).astype(jnp.float32) * HD ** (-0.5)
    row_weights = jnp.repeat((level_weight * used).swapaxes(0, 1), GROUP, axis=1)
    head_normed = pl.pallas_call(
        functools.partial(head_kernel, local_bits),
        grid=(heads_here,),
        in_specs=[
            pl.BlockSpec((1, tok_rows, HD), functools.partial(head_block, k)) for k in range(3)
        ]
        + [
            pl.BlockSpec((1,) + row_weights.shape[1:], lambda h: (h, 0, 0)),
            pl.BlockSpec((seq_bits, 1, HD, HD), lambda h: (0, h, 0, 0)),
            pl.BlockSpec((1, HD), lambda h: (0, h)),
        ],
        out_specs=pl.BlockSpec((tok_rows, HD), lambda h: (0, h)),
        out_shape=jax.ShapeDtypeStruct((tok_rows, heads_here * HD), jnp.bfloat16),
        compiler_params=pltpu.CompilerParams(vmem_limit_bytes=32 * 2**20),
        cost_estimate=pl.CostEstimate(
            flops=heads_here * tok_rows * HD * 4 * (tok_rows + HD * seq_bits),
            bytes_accessed=tok_rows * heads_here * HD * 12,
            transcendentals=0,
        ),
    )(projected, projected, projected, row_weights, jnp.stack(partners), head_gain[None, :])
    axes = ("head", "sub")
    shares = lax.axis_size(axes)
    feature_cols = out_matrix.shape[0] // shares
    mine = lax.axis_index(axes)

    def terms(share):
        part = lax.dynamic_slice_in_dim(out_matrix, share * feature_cols, feature_cols, 0)
        return lax.dot_general(
            head_normed, part, (((1,), (1,)), ((), ())), preferred_element_type=jnp.float32
        )

    residual = lax.dynamic_slice_in_dim(widened, mine * feature_cols, feature_cols, 1)
    if shares == 2:
        theirs = terms(1 - mine).astype(jnp.bfloat16)
        arrived = lax.ppermute(theirs, axes, [(0, 1), (1, 0)])
        summed = terms(mine) + arrived.astype(jnp.float32)
    else:
        local_terms = lax.dot_general(
            head_normed, out_matrix, (((1,), (1,)), ((), ())), preferred_element_type=jnp.float32
        )
        summed = lax.psum_scatter(
            local_terms.astype(jnp.bfloat16), axes, scatter_dimension=1, tiled=True
        ).astype(jnp.float32)
    return (residual + summed).astype(jnp.bfloat16)


def solution(mesh):
    placed = (
        P(("doc", "seq"), None),
        P(),
        P(None, "seq", ("head", "sub")),
        P(("doc", "seq"), ("head", "sub"), None),
        P(("head", "sub")),
        P(("head", "sub"), "seq"),
    )
    return jax.shard_map(
        body,
        mesh=mesh,
        in_specs=placed,
        out_specs=P(("doc", "seq"), ("head", "sub")),
        check_vma=False,
    )
```
